512 devices in a mesh: replica: 64 (over x, z_lo, y), tensor: 8 (over z_hi, core).
Axes of the slice: x: 4, y: 4, z: 16 (z_hi: 4, z_lo: 4; z = z_hi * 4 + z_lo), core: 2. Of those that a mesh axis runs over, the one named last changes fastest.
Arguments:
- hidden: bfloat16 [8, 2048, 8192], P(None, 'replica', 'tensor'), may hold values from -6 to 6
- kv_weight: bfloat16 [2048, 8192], P('replica', 'tensor'), may hold values from -0.0625 to 0.0625
- owner: int32 [64], replicated, may hold values from 0 to 63, each once
- queries: bfloat16 [8, 2048, 8192], P(None, 'replica', 'tensor'), may hold values from -160 to 160
- pool: bfloat16 [12288, 16, 2048], P('replica', None, 'tensor'), may hold values from -17 to 17
- page_table: int32 [2048, 6], P('replica'), may hold values from 0 to 319, as said below
- lengths: int32 [2048], P('replica'), may hold values from 1 to 96
- send_pages: int32 [64, 64, 2], P('replica'), may hold values from 0 to 191, as said below
Outputs:
- new_kv: bfloat16 [8, 2048, 2048], P(None, 'replica', 'tensor')
- attended: bfloat16 [8, 2048, 8192], P(None, 'replica', 'tensor')
The draws below stay inside these ranges and needn't reach their ends.
Inputs may be any that keep to these rules, and one draw needn't show every extreme that they name: `page_table`: entry e < 192 names page e of the home replica's own pool; otherwise the page in slot (e - 192) % 2 of the list that replica (e - 192) // 2 sends to the home replica. Only the first ceil(lengths / 16) entries of a row are read. send_pages[j, h] names pages by their index within replica j's own 192 pages.
All inputs are finite; a program needn't handle non-finite values.
Results may differ from the reference program's by a relative error of at most 0.0044.
Values may be sent and summed in bfloat16 or wider, within the bound.
No kernel may reach another device: no remote copies, remote signals or barrier semaphores. Data moves between devices by JAX's collectives and lax.ppermute only.
A program may use at most 64 MiB of HBM per device.

```python
import jax
import jax.numpy as jnp
from jax import lax

D = 8192
QH = 64
KVH = 8
HD = 128
PAGE = 16
MAXP = 6
CAP = 2
STEPS = 8
SEQ_DEV = 32
KV_COLS = 2048
SEQS = 2048
PPD = 192
N_REPLICA = 64


def migration_plan(key):
    resident_count = PPD - N_REPLICA * CAP
    streams = jax.random.split(key, 6)
    orders = jax.vmap(lambda subkey: jax.random.permutation(subkey, PPD))(jax.random.split(streams[0], N_REPLICA)).astype(jnp.int32)
    popular = jax.random.randint(streams[1], (N_REPLICA,), 0, 4) == 0
    forced = jax.random.randint(streams[2], (), 0, N_REPLICA)
    popular = jnp.logical_or(popular, jnp.arange(N_REPLICA) == forced)
    counts = jax.random.randint(streams[3], (N_REPLICA, N_REPLICA), 0, CAP + 1)
    counts = jnp.where(popular[None, :], CAP, counts)
    send_slots = orders[:, :N_REPLICA * CAP].reshape(N_REPLICA, N_REPLICA, CAP)
    arrived = PPD + jnp.arange(N_REPLICA * CAP, dtype=jnp.int32)

    def per_home(home, subkey):
        candidates = jnp.concatenate([orders[home][N_REPLICA * CAP:], arrived])
        used = jnp.arange(CAP)[None, :] < counts[:, home][:, None]
        valid = jnp.concatenate([jnp.ones((resident_count,), jnp.bool_), used.reshape(-1)])
        shuffle = jax.random.permutation(subkey, PPD).astype(jnp.int32)
        score = jnp.where(valid, 0, PPD) + shuffle
        ranked = candidates[jnp.argsort(score)]
        total = jnp.sum(valid.astype(jnp.int32))
        table = ranked.reshape(MAXP, SEQ_DEV).T
        pages = jnp.clip((total - jnp.arange(SEQ_DEV) + SEQ_DEV - 1) // SEQ_DEV, 1, MAXP)
        return (table, pages)
    tables, pages = jax.vmap(per_home)(jnp.arange(N_REPLICA), jax.random.split(streams[4], N_REPLICA))
    shorten = jax.random.randint(streams[5], (N_REPLICA, SEQ_DEV), 0, PAGE)
    shorten = jnp.where(jnp.arange(SEQ_DEV)[None, :] == 0, 0, shorten)
    seq_lengths = pages * PAGE - shorten
    return (tables.reshape(N_REPLICA * SEQ_DEV, MAXP).astype(jnp.int32), seq_lengths.reshape(-1).astype(jnp.int32), send_slots.astype(jnp.int32))


def draw_page_table(key, part):
    return migration_plan(key)[0]


def draw_lengths(key, part):
    return migration_plan(key)[1]


def draw_send_pages(key, part):
    return migration_plan(key)[2]


def draw_queries(key, part):
    key = jax.random.fold_in(key, 11)
    shape = (STEPS, SEQ_DEV * N_REPLICA, QH * HD)
    return jnp.clip(jax.random.normal(key, shape, jnp.float32), -6.0, 6.0).astype(jnp.bfloat16)


def draw_pool(key, part):
    key = jax.random.fold_in(key, 12)
    shape = (N_REPLICA * PPD, PAGE, KV_COLS)
    return jnp.clip(jax.random.normal(key, shape, jnp.float32), -6.0, 6.0).astype(jnp.bfloat16)


def block_levels(key, extent, cuts, smallest, high):
    gain = 1.0
    for position, parts in cuts:
        steps = jax.random.uniform(jax.random.fold_in(jax.random.fold_in(key, 6), position), (parts,), jnp.float32, smallest / len(cuts), high / len(cuts))
        gain = gain * jnp.repeat(jnp.exp(steps), extent[position] // parts).reshape((-1,) + (1,) * (len(extent) - 1 - position))
    return gain


def centred(key, extent, deviation, limit, cuts=(), kind=jnp.bfloat16):
    values = jax.random.normal(key, extent, jnp.float32) * deviation
    if len(cuts) > 0:
        values = block_levels(key, extent, cuts, -0.22, 0.18) * values
    return jnp.clip(values, min=-limit, max=limit).astype(kind)


def setup_inputs(seed: int = 0) -> dict:
    key_list = jax.random.split(jax.random.key(seed), 9)
    return {
        "hidden": centred(key_list[0], (STEPS, SEQS, D), 1.0, 6.0, ((1, 64), (2, 8))),
        "kv_weight": centred(key_list[1], (KV_COLS, D), D ** -0.5, 0.0625, ((0, 64), (1, 8))),
        "owner": jax.random.permutation(key_list[2], N_REPLICA).astype(jnp.int32),
        "queries": draw_queries(jax.random.fold_in(key_list[8], 71), 0),
        "pool": draw_pool(jax.random.fold_in(key_list[8], 71), 0),
        "page_table": draw_page_table(jax.random.fold_in(key_list[8], 71), 0),
        "lengths": draw_lengths(jax.random.fold_in(key_list[8], 71), 0),
        "send_pages": draw_send_pages(jax.random.fold_in(key_list[8], 71), 0),
    }


def attend(query_rows, cache, fresh, seq_lengths):
    steps_count, seq_count, width = query_rows.shape
    group = QH // KVH
    span = cache.shape[1]
    query = query_rows.astype(jnp.float32).reshape(steps_count, seq_count, KVH, group, HD)
    cache = cache.astype(jnp.float32).reshape(seq_count, span, KVH, 2, HD)
    fresh = fresh.astype(jnp.float32).reshape(steps_count, seq_count, KVH, 2, HD)
    scale = HD ** -0.5
    past = jnp.einsum("tshgd,schd->tshgc", query, cache[:, :, :, 0]) * scale
    recent = jnp.einsum("tshgd,ushd->tshgu", query, fresh[:, :, :, 0]) * scale
    live = jnp.arange(span)[None, :] < seq_lengths[:, None]
    past = jnp.where(live[None, :, None, None, :], past, -jnp.inf)
    causal = jnp.arange(steps_count)[None, :] <= jnp.arange(steps_count)[:, None]
    recent = jnp.where(causal[:, None, None, None, :], recent, -jnp.inf)
    top = jnp.maximum(jnp.max(past, -1), jnp.max(recent, -1))[..., None]
    past_w = jnp.exp(past - top)
    recent_w = jnp.exp(recent - top)
    total = jnp.sum(past_w, -1) + jnp.sum(recent_w, -1)
    past_b = lax.optimization_barrier(past_w.astype(jnp.bfloat16)).astype(jnp.float32)
    recent_b = lax.optimization_barrier(recent_w.astype(jnp.bfloat16)).astype(jnp.float32)
    mixed = jnp.einsum("tshgc,schd->tshgd", past_b, cache[:, :, :, 1])
    mixed = mixed + jnp.einsum("tshgu,ushd->tshgd", recent_b, fresh[:, :, :, 1])
    result = mixed / total[..., None]
    return result.reshape(steps_count, seq_count, width).astype(jnp.bfloat16)


def reference(hidden, kv_weight, owner, queries, pool, page_table, lengths, send_pages):
    blocks = kv_weight.reshape(N_REPLICA, KV_COLS // N_REPLICA, D)
    weight = blocks[owner].reshape(KV_COLS, D)
    fresh_all = jnp.dot(hidden.reshape(STEPS * SEQS, D), weight.T, preferred_element_type=jnp.float32)
    new_kv = fresh_all.astype(jnp.bfloat16).reshape(STEPS, SEQS, KV_COLS)

    def one_replica(home):
        table = lax.dynamic_slice_in_dim(page_table, home * SEQ_DEV, SEQ_DEV, 0)
        seq_lengths = lax.dynamic_slice_in_dim(lengths, home * SEQ_DEV, SEQ_DEV, 0)
        query_rows = lax.dynamic_slice_in_dim(queries, home * SEQ_DEV, SEQ_DEV, 1)
        fresh = lax.dynamic_slice_in_dim(new_kv, home * SEQ_DEV, SEQ_DEV, 1)
        remote = jnp.maximum(table - PPD, 0)
        source = (remote // CAP).astype(jnp.int32)
        slot = (remote % CAP).astype(jnp.int32)
        far_page = send_pages[source, home, slot]
        rows_global = jnp.where(table < PPD, home * PPD + table, source * PPD + far_page).astype(jnp.int32)
        cache = pool[rows_global].reshape(SEQ_DEV, MAXP * PAGE, KV_COLS)
        return attend(query_rows, cache, fresh, seq_lengths)

    outputs = lax.map(one_replica, jnp.arange(N_REPLICA, dtype=jnp.int32))
    attended = jnp.transpose(outputs, (1, 0, 2, 3)).reshape(STEPS, SEQS, QH * HD)
    return new_kv, attended
```

```python
import jax
import jax.numpy as jnp
from jax import lax
from jax.experimental import pallas as pl
from jax.experimental.pallas import tpu as pltpu
from jax.sharding import Mesh, PartitionSpec as P

HD = 128
SIDE = 4
CORES = 2
AXES = ("x", "zl", "y", "zh", "c")
REPLICA = ("x", "zl", "y")
TENSOR = ("zh", "c")
RING = range(SIDE)


def flat_id(x, zl, y, zh, c):
    return (((x * SIDE + zl) * SIDE + y) * SIDE + zh) * CORES + c


def member(stage, c, line, k, zl, zh):
    along_y = (c == 0) == (stage == 1)
    return flat_id(line, zl, k, zh, c) if along_y else flat_id(k, zl, line, zh, c)


def lines(stage):
    return [
        [member(stage, c, line, k, zl, zh) for k in RING]
        for line in RING for zl in RING for zh in RING for c in range(CORES)
    ]


def shift(value, stage, step):
    pairs = [
        (group[k], group[(k + step) % SIDE]) for group in lines(stage) for k in RING
    ]
    return lax.ppermute(value, AXES, pairs)


def z_shift(value, step):
    return lax.ppermute(value, "zh", [(i, (i + step) % SIDE) for i in RING])


def core_swap(value):
    return lax.ppermute(value, "c", [(0, 1), (1, 0)])


def gather_weight(held):
    first = lax.all_to_all(
        jnp.broadcast_to(held[None], (SIDE,) + held.shape), "zl", 0, 0, tiled=True
    )
    block = first.reshape((1, SIDE * held.shape[0], held.shape[1]))
    second = lax.all_to_all(
        jnp.broadcast_to(block, (SIDE,) + block.shape[1:]),
        AXES, 0, 0, axis_index_groups=lines(1),
    )
    own = second.reshape(-1, held.shape[1])
    half = own.shape[0] // 2
    up = shift(own, 2, 1)
    down = shift(own, 2, -1)
    far_up = shift(up[:half], 2, 1)
    far_down = shift(down[half:], 2, -1)
    return own, up, down, far_up, far_down


def block_places(owner, c, q):
    x, y = lax.axis_index("x"), lax.axis_index("y")
    place = jnp.arange(64)
    slot, a1, zl = place // 16, (place // 4) % 4, place % 4
    me2 = jnp.where(c == 0, x, y)
    a2 = (me2 + jnp.where(slot == 0, 0, jnp.where(slot == 1, 3, jnp.where(slot == 2, 1, 2)))) % 4
    held = jnp.where(c == 0, a2 * 16 + zl * 4 + a1, a1 * 16 + zl * 4 + a2)
    block = jnp.sum(jnp.where(owner[None, :] == held[:, None], jnp.arange(64)[None, :], 0), axis=1)
    column = block // 8
    far = (column // 2 - q) % 4
    order = jnp.where(far == 2, 0, jnp.where(far == 1, 1, jnp.where(far == 3, 2, 3)))
    order = order + jnp.where(column % 2 == c, 4, 0)
    return (order * 8 + block % 8).astype(jnp.int32)


def project_kernel(places, rows, own, up, down, far_up, far_down, first, rest, mine, total, sems):
    base = 0
    for piece in (own, up, down, far_up, far_down):
        count = piece.shape[0] // 32
        product = lax.dot_general(
            piece[...], rows[...], (((1,), (1,)), ((), ())), preferred_element_type=jnp.float32
        )
        for b in range(count):
            at = pl.multiple_of(places[base + b] * 32, 32)
            total[pl.ds(at, 32), :] = product[b * 32:(b + 1) * 32]
        base += count
    copies = [
        pltpu.make_async_copy(total.at[pl.ds(0, 256)], first, sems.at[0]),
        pltpu.make_async_copy(total.at[pl.ds(256, 768)], rest, sems.at[1]),
        pltpu.make_async_copy(total.at[pl.ds(1024, 1024)], mine, sems.at[2]),
    ]
    for copy in copies:
        copy.start()
    for copy in copies:
        copy.wait()


def project(places, rows, pieces):
    count = rows.shape[0]
    vmem = pl.BlockSpec(memory_space=pltpu.VMEM)
    return pl.pallas_call(
        project_kernel,
        out_shape=[
            jax.ShapeDtypeStruct((256, count), jnp.float32),
            jax.ShapeDtypeStruct((768, count), jnp.float32),
            jax.ShapeDtypeStruct((1024, count), jnp.float32),
        ],
        in_specs=[pl.BlockSpec(memory_space=pltpu.SMEM)] + [vmem] * 6,
        out_specs=[pl.BlockSpec(memory_space=pl.ANY)] * 3,
        scratch_shapes=[
            pltpu.VMEM((2048, count), jnp.float32),
            pltpu.SemaphoreType.DMA((3,)),
        ],
        compiler_params=pltpu.CompilerParams(vmem_limit_bytes=24 * 2**20),
        name="project",
    )(places, rows, *pieces)


def reduce_columns(first, rest, mine):
    far = mine[:256] + core_swap(first)
    near = mine[256:] + core_swap(rest)
    up, down, here = near[:256], near[256:512], near[512:]
    via_up = z_shift(far[:128], 1)
    via_down = z_shift(far[128:], -1)
    up_v = z_shift(up[128:], 1)
    down_k = z_shift(down[:128], -1)
    up_k = z_shift(up[:128] + via_up, 1)
    down_v = z_shift(down[128:] + via_down, -1)
    return here + jnp.concatenate([up_k, up_v], 0) + jnp.concatenate([down_k, down_v], 0)


def attend(query_rows, cache, fresh, seq_lengths):
    steps_count, seq_count, width = query_rows.shape
    kv_heads = cache.shape[-1] // (2 * HD)
    group = width // (HD * kv_heads)
    span = cache.shape[1]
    query = query_rows.reshape(steps_count, seq_count, kv_heads, group, HD)
    cache = cache.reshape(seq_count, span, kv_heads, 2, HD)
    fresh = fresh.reshape(steps_count, seq_count, kv_heads, 2, HD)
    scale = HD ** (-0.5)
    past = (
        jnp.einsum(
            "tshgd,schd->tshgc", query, cache[:, :, :, 0], preferred_element_type=jnp.float32
        )
        * scale
    )
    recent = (
        jnp.einsum(
            "tshgd,ushd->tshgu", query, fresh[:, :, :, 0], preferred_element_type=jnp.float32
        )
        * scale
    )
    live = jnp.arange(span)[None, :] < seq_lengths[:, None]
    past = jnp.where(live[None, :, None, None, :], past, -jnp.inf)
    causal = jnp.arange(steps_count)[None, :] <= jnp.arange(steps_count)[:, None]
    recent = jnp.where(causal[:, None, None, None, :], recent, -jnp.inf)
    top = jnp.maximum(jnp.max(past, -1), jnp.max(recent, -1))[..., None]
    past_w = jnp.exp(past - top)
    recent_w = jnp.exp(recent - top)
    total = jnp.sum(past_w, -1) + jnp.sum(recent_w, -1)
    mixed = jnp.einsum(
        "tshgc,schd->tshgd",
        past_w.astype(jnp.bfloat16),
        cache[:, :, :, 1],
        preferred_element_type=jnp.float32,
    )
    mixed = mixed + jnp.einsum(
        "tshgu,ushd->tshgd",
        recent_w.astype(jnp.bfloat16),
        fresh[:, :, :, 1],
        preferred_element_type=jnp.float32,
    )
    result = mixed / total[..., None]
    return result.reshape(steps_count, seq_count, width).astype(jnp.bfloat16)


def on_device(hidden, kv_weight, owner, queries, pool, page_table, lengths, send_pages):
    steps_count, seq_count, feature_part = hidden.shape
    page_size, kv_width = pool.shape[1:]
    c, q = lax.axis_index("c"), lax.axis_index("zh")
    outgoing = jnp.take(pool, send_pages.reshape(-1), axis=0, mode="clip").reshape(
        64, -1, page_size, kv_width
    )
    arrived = lax.all_to_all(outgoing, REPLICA, split_axis=0, concat_axis=0, tiled=True)

    pieces = gather_weight(kv_weight)
    places = block_places(owner, c, q)
    first, rest, mine = project(places, hidden.reshape(-1, feature_part), pieces)
    fresh = reduce_columns(first, rest, mine)
    new_kv = fresh.T.astype(jnp.bfloat16).reshape(steps_count, seq_count, kv_width)

    store = jnp.concatenate([pool, arrived.reshape(-1, page_size, kv_width)], axis=0)
    cache = jnp.take(store, page_table.reshape(-1), axis=0, mode="clip").reshape(seq_count, -1, kv_width)
    attended = attend(queries, cache, new_kv, lengths)
    return (new_kv, attended)


def solution(mesh):
    fine = Mesh(mesh.devices.reshape(SIDE, SIDE, SIDE, SIDE, CORES), AXES)
    in_specs = (
        P(None, REPLICA, TENSOR),
        P(REPLICA, TENSOR),
        P(),
        P(None, REPLICA, TENSOR),
        P(REPLICA, None, TENSOR),
        P(REPLICA, None),
        P(REPLICA),
        P(REPLICA, None, None),
    )
    out_specs = (P(None, REPLICA, TENSOR), P(None, REPLICA, TENSOR))
    return jax.shard_map(
        on_device, mesh=fine, in_specs=in_specs, out_specs=out_specs, check_vma=False
    )
```

```python
import jax
import jax.numpy as jnp
from jax import lax
from jax.experimental import pallas as pl
from jax.experimental.pallas import tpu as pltpu
from jax.sharding import Mesh, PartitionSpec as P

HD = 128
SIDE = 4
CORES = 2
SCALE = 16.0
SPAN = 96
WIDE = 128
AXES = ("x", "zl", "y", "zh", "c")
REPLICA = ("x", "zl", "y")
TENSOR = ("zh", "c")
RING = range(SIDE)


def flat_id(x, zl, y, zh, c):
    return (((x * SIDE + zl) * SIDE + y) * SIDE + zh) * CORES + c


def member(stage, c, line, k, zl, zh):
    along_y = (c == 0) == (stage == 1)
    return flat_id(line, zl, k, zh, c) if along_y else flat_id(k, zl, line, zh, c)


def lines(stage):
    return [
        [member(stage, c, line, k, zl, zh) for k in RING]
        for line in RING for zl in RING for zh in RING for c in range(CORES)
    ]


def shift(value, stage, step):
    pairs = [
        (group[k], group[(k + step) % SIDE]) for group in lines(stage) for k in RING
    ]
    return lax.ppermute(value, AXES, pairs)


def partner(zh, c, step):
    return zh ^ 1 if (c == 0) == (step == 1) else SIDE - 1 - zh


def z_exchange(value, step):
    pairs = [
        (zh * CORES + c, partner(zh, c, step) * CORES + c) for zh in RING for c in range(CORES)
    ]
    sent = (value * SCALE).astype(jnp.float16)
    return lax.ppermute(sent, TENSOR, pairs).astype(jnp.float32) * (1.0 / SCALE)


def core_swap(value):
    return lax.ppermute(value, "c", [(0, 1), (1, 0)])


def gather_weight(held):
    first = lax.all_to_all(
        jnp.broadcast_to(held[None], (SIDE,) + held.shape), "zl", 0, 0, tiled=True
    )
    block = first.reshape((1, SIDE * held.shape[0], held.shape[1]))
    second = lax.all_to_all(
        jnp.broadcast_to(block, (SIDE,) + block.shape[1:]),
        AXES, 0, 0, axis_index_groups=lines(1),
    )
    own = second.reshape(-1, held.shape[1])
    half = own.shape[0] // 2
    up_on, down_on = shift(own[:half], 2, 1), shift(own[half:], 2, -1)
    up_end, down_end = shift(own[half:], 2, 1), shift(own[:half], 2, -1)
    far_up, far_down = shift(up_on, 2, 1), shift(down_on, 2, -1)
    return own, up_on, up_end, down_end, down_on, far_up, far_down


def block_places(owner, c, q):
    x, y = lax.axis_index("x"), lax.axis_index("y")
    place = jnp.arange(64)
    slot, a1, zl = place // 16, (place // 4) % 4, place % 4
    me2 = jnp.where(c == 0, x, y)
    a2 = (me2 + jnp.where(slot == 0, 0, jnp.where(slot == 1, 3, jnp.where(slot == 2, 1, 2)))) % 4
    held = jnp.where(c == 0, a2 * 16 + zl * 4 + a1, a1 * 16 + zl * 4 + a2)
    block = jnp.sum(jnp.where(owner[None, :] == held[:, None], jnp.arange(64)[None, :], 0), axis=1)
    column = block // 8
    target, core = column // 2, column % 2
    order = jnp.where((target == (q ^ 1)) == (core == 0), 1, 2)
    order = jnp.where(target == q, 3, jnp.where(target == (q + 2) % 4, 0, order))
    order = order + jnp.where(core == c, 4, 0)
    return (order * 8 + block % 8).astype(jnp.int32)


def project_kernel(places, rows, own, up_on, up_end, down_end, down_on, far_up, far_down, away, near, late, total, sems):
    base = 0
    for piece in (own, up_on, up_end, down_end, down_on, far_up, far_down):
        count = piece.shape[0] // 32
        product = lax.dot_general(
            piece[...], rows[...], (((1,), (1,)), ((), ())), preferred_element_type=jnp.float32
        )
        for b in range(count):
            at = pl.multiple_of(places[base + b] * 32, 32)
            total[pl.ds(at, 32), :] = product[b * 32:(b + 1) * 32]
        base += count
    copies, base = [], 0
    for i, out in enumerate((away, near, late)):
        copies.append(pltpu.make_async_copy(total.at[pl.ds(base, out.shape[0])], out, sems.at[i]))
        base += out.shape[0]
    for copy in copies:
        copy.start()
    for copy in copies:
        copy.wait()


def project(places, rows, pieces):
    count = rows.shape[0]
    vmem = pl.BlockSpec(memory_space=pltpu.VMEM)
    return pl.pallas_call(
        project_kernel,
        out_shape=[
            jax.ShapeDtypeStruct((size, count), jnp.float32) for size in (1024, 512, 512)
        ],
        in_specs=[pl.BlockSpec(memory_space=pltpu.SMEM)] + [vmem] * 8,
        out_specs=[pl.BlockSpec(memory_space=pl.ANY)] * 3,
        scratch_shapes=[
            pltpu.VMEM((2048, count), jnp.float32),
            pltpu.SemaphoreType.DMA((3,)),
        ],
        compiler_params=pltpu.CompilerParams(vmem_limit_bytes=24 * 2**20),
        name="project",
    )(places, rows, *pieces)


def reduce_columns(away, near, late):
    got = core_swap(away)
    got_near = z_exchange(near + got[:512], 1)
    got_late = z_exchange(late[:256] + got[512:768] + got_near[:256], 2)
    return got, (late[256:], got[768:], got_near[256:], got_late)


def past_kernel(table, lengths, queries, pool, arrived, scores, folded, values, cells, wide):
    steps, seqs, _ = queries.shape
    pages = pool.shape[0]

    def fetch(s, _):
        for e in range(SPAN // 16):
            entry = table[s * (SPAN // 16) + e]
            mine = pool[jnp.minimum(entry, pages - 1)]
            sent = arrived[jnp.maximum(entry - pages, 0)]
            cells[s, e * 16:(e + 1) * 16] = jnp.where(entry < pages, mine, sent)
        return 0

    lax.fori_loop(0, seqs, fetch, 0, unroll=2)
    cells[:, SPAN:, :] = jnp.zeros((seqs, WIDE - SPAN, cells.shape[2]), cells.dtype)
    for t in range(steps):
        for h in range(8):
            wide[h, pl.ds(t * seqs, seqs), :] = queries[t, :, h * HD:(h + 1) * HD].astype(jnp.float32)
    for s in range(seqs):
        folded[s] = jnp.concatenate(
            [wide[h, pl.ds(s, steps, stride=seqs), :] for h in range(8)], axis=0
        ).astype(jnp.bfloat16)
    column = lax.broadcasted_iota(jnp.int32, (64, WIDE), 1)
    for s in range(seqs):
        scores[s] = lax.dot_general(
            folded[s], cells[s, :, :HD], (((1,), (1,)), ((), ())),
            preferred_element_type=jnp.float32,
        ) * (HD ** -0.5)
    for s in range(seqs):
        live = (column < lengths[s]) | (column >= SPAN)
        scores[s] = jnp.where(live, scores[s], -jnp.inf)
    for s in range(seqs):
        values[s] = cells[s, :, HD:]


def past(table, lengths, queries, pool, arrived):
    steps, seqs, _ = queries.shape
    smem = pl.BlockSpec(memory_space=pltpu.SMEM)
    vmem = pl.BlockSpec(memory_space=pltpu.VMEM)
    return pl.pallas_call(
        past_kernel,
        out_shape=[
            jax.ShapeDtypeStruct((seqs, 64, WIDE), jnp.float32),
            jax.ShapeDtypeStruct((seqs, 64, HD), jnp.bfloat16),
            jax.ShapeDtypeStruct((seqs, WIDE, HD), jnp.bfloat16),
        ],
        in_specs=[smem, smem, vmem, vmem, vmem],
        out_specs=[vmem, vmem, vmem],
        scratch_shapes=[
            pltpu.VMEM((seqs, WIDE, 2 * HD), jnp.bfloat16),
            pltpu.VMEM((8, steps * seqs, HD), jnp.float32),
        ],
        compiler_params=pltpu.CompilerParams(vmem_limit_bytes=24 * 2**20),
        cost_estimate=pl.CostEstimate(flops=70_000_000, bytes_accessed=8_000_000, transcendentals=0),
        name="past",
    )(table, lengths, queries, pool, arrived)


def finish_kernel(*refs):
    *parts, scores, folded, values, new_kv, attended, wide, keys, mixed, weights, totals, own = refs
    seqs = scores.shape[0]
    steps = new_kv.shape[0]
    fresh = parts[0][...].astype(jnp.float32)
    for part in parts[1:]:
        fresh = fresh + part[...].astype(jnp.float32)
    fresh = fresh.T.astype(jnp.bfloat16)
    for t in range(steps):
        new_kv[t] = fresh[t * seqs:(t + 1) * seqs]
    wide[0] = fresh[:, :HD].astype(jnp.float32)
    wide[1] = fresh[:, HD:].astype(jnp.float32)
    lanes = lax.broadcasted_iota(jnp.int32, (64, WIDE), 1)
    step = lax.broadcasted_iota(jnp.int32, (64, WIDE), 0) % steps
    later = (lanes - SPAN) > step
    zeros = jnp.zeros((16 - steps, HD), jnp.float32)
    keys[...] = jnp.zeros(keys.shape, keys.dtype)
    for s in range(seqs):
        key, value = (
            jnp.concatenate([wide[i, pl.ds(s, steps, stride=seqs), :], zeros], axis=0)
            for i in range(2)
        )
        keys[s, pl.ds(SPAN, 16), :] = key.astype(jnp.bfloat16)
        own[s] = value.astype(jnp.bfloat16)
    for s in range(seqs):
        recent = lax.dot_general(
            folded[s], keys[s], (((1,), (1,)), ((), ())), preferred_element_type=jnp.float32
        ) * (HD ** -0.5)
        mixed[pl.ds(s * 64, 64), :] = jnp.where(later, -jnp.inf, scores[s] + recent)
    for s in range(seqs):
        score = mixed[pl.ds(s * 64, 64), :]
        weight = jnp.exp(score - jnp.max(score, axis=1, keepdims=True))
        weights[s] = weight.astype(jnp.bfloat16)
        totals[s] = jnp.broadcast_to(jnp.sum(weight, axis=1, keepdims=True), (64, HD))
    for s in range(seqs):
        value = jnp.concatenate([values[s, :SPAN], own[s], values[s, SPAN + 16:]], axis=0)
        out = lax.dot_general(
            weights[s], value, (((1,), (0,)), ((), ())), preferred_element_type=jnp.float32
        )
        mixed[pl.ds(s * 64, 64), :] = out / totals[s]
    for t in range(steps):
        for h in range(8):
            attended[t, :, h * HD:(h + 1) * HD] = mixed[
                pl.ds(h * steps + t, seqs, stride=64), :
            ].astype(jnp.bfloat16)


def finish(parts, scores, folded, values, steps):
    seqs = scores.shape[0]
    vmem = pl.BlockSpec(memory_space=pltpu.VMEM)
    return pl.pallas_call(
        finish_kernel,
        out_shape=[
            jax.ShapeDtypeStruct((steps, seqs, 2 * HD), jnp.bfloat16),
            jax.ShapeDtypeStruct((steps, seqs, 8 * HD), jnp.bfloat16),
        ],
        in_specs=[vmem] * (len(parts) + 3),
        out_specs=[vmem, vmem],
        scratch_shapes=[
            pltpu.VMEM((2, steps * seqs, HD), jnp.float32),
            pltpu.VMEM((seqs, WIDE, HD), jnp.bfloat16),
            pltpu.VMEM((seqs * 64, HD), jnp.float32),
            pltpu.VMEM((seqs, 64, WIDE), jnp.bfloat16),
            pltpu.VMEM((seqs, 64, HD), jnp.float32),
            pltpu.VMEM((seqs, 16, HD), jnp.bfloat16),
        ],
        compiler_params=pltpu.CompilerParams(vmem_limit_bytes=24 * 2**20),
        cost_estimate=pl.CostEstimate(flops=140_000_000, bytes_accessed=4_000_000, transcendentals=262144),
        name="finish",
    )(*parts, scores, folded, values)


def on_device(hidden, kv_weight, owner, queries, pool, page_table, lengths, send_pages):
    steps_count, _, feature_part = hidden.shape
    page_size, kv_width = pool.shape[1:]
    c, q = lax.axis_index("c"), lax.axis_index("zh")
    outgoing = jnp.take(pool, send_pages.reshape(-1), axis=0, mode="clip").reshape(
        64, -1, page_size, kv_width
    )
    arrived = lax.all_to_all(outgoing, REPLICA, split_axis=0, concat_axis=0, tiled=True)

    pieces, arrived = lax.optimization_barrier((gather_weight(kv_weight), arrived))
    places = block_places(owner, c, q)
    swapped, parts = reduce_columns(*project(places, hidden.reshape(-1, feature_part), pieces))
    queries, _ = lax.optimization_barrier((queries, swapped))
    scores, folded, values = past(
        page_table.reshape(-1), lengths, queries, pool, arrived.reshape(-1, page_size, kv_width)
    )
    return tuple(finish(parts, scores, folded, values, steps_count))


def solution(mesh):
    fine = Mesh(mesh.devices.reshape(SIDE, SIDE, SIDE, SIDE, CORES), AXES)
    in_specs = (
        P(None, REPLICA, TENSOR),
        P(REPLICA, TENSOR),
        P(),
        P(None, REPLICA, TENSOR),
        P(REPLICA, None, TENSOR),
        P(REPLICA, None),
        P(REPLICA),
        P(REPLICA, None, None),
    )
    out_specs = (P(None, REPLICA, TENSOR), P(None, REPLICA, TENSOR))
    return jax.shard_map(
        on_device, mesh=fine, in_specs=in_specs, out_specs=out_specs, check_vma=False
    )
```

```python
import jax
import jax.numpy as jnp
from jax import lax
from jax.experimental import pallas as pl
from jax.experimental.pallas import tpu as pltpu
from jax.sharding import Mesh, PartitionSpec as P

HD = 128
SIDE = 4
CORES = 2
SCALE = 16.0
SPAN = 96
WIDE = 128
AXES = ("x", "zl", "y", "zh", "c")
REPLICA = ("x", "zl", "y")
TENSOR = ("zh", "c")
RING = range(SIDE)


def flat_id(x, zl, y, zh, c):
    return (((x * SIDE + zl) * SIDE + y) * SIDE + zh) * CORES + c


def member(stage, c, line, k, zl, zh):
    along_y = (c == 0) == (stage == 1)
    return flat_id(line, zl, k, zh, c) if along_y else flat_id(k, zl, line, zh, c)


def lines(stage):
    return [
        [member(stage, c, line, k, zl, zh) for k in RING]
        for line in RING for zl in RING for zh in RING for c in range(CORES)
    ]


def shift(value, stage, step):
    pairs = [
        (group[k], group[(k + step) % SIDE]) for group in lines(stage) for k in RING
    ]
    return lax.ppermute(value, AXES, pairs)


def partner(zh, c, step):
    return zh ^ 1 if (c == 0) == (step == 1) else SIDE - 1 - zh


def z_exchange(value, step):
    pairs = [
        (zh * CORES + c, partner(zh, c, step) * CORES + c) for zh in RING for c in range(CORES)
    ]
    return lax.ppermute((value * SCALE).astype(jnp.float16), TENSOR, pairs)


def unscaled(value):
    return value.astype(jnp.float32) * (1.0 / SCALE)


def core_swap(value):
    return lax.ppermute(value, "c", [(0, 1), (1, 0)])


def gather_weight(held, outgoing):
    first = lax.all_to_all(
        jnp.broadcast_to(held[None], (SIDE,) + held.shape), "zl", 0, 0, tiled=True
    )
    block = first.reshape((1, SIDE * held.shape[0], held.shape[1]))
    second = lax.all_to_all(
        jnp.broadcast_to(block, (SIDE,) + block.shape[1:]),
        AXES, 0, 0, axis_index_groups=lines(1),
    )
    second, outgoing = lax.optimization_barrier((second, outgoing))
    own = second.reshape(-1, held.shape[1])
    half = own.shape[0] // 2
    low, high = own[:half], own[half:]
    up_on, down_on = shift(low, 2, 1), shift(high, 2, -1)
    up_end, down_end = shift(high, 2, 1), shift(low, 2, -1)
    far_up, far_down = shift(up_on, 2, 1), shift(down_on, 2, -1)
    return outgoing, (low, high, up_on, up_end, down_end, down_on, far_up, far_down)


def block_places(owner, c, q):
    x, y = lax.axis_index("x"), lax.axis_index("y")
    place = jnp.arange(64)
    slot, a1, zl = place // 16, (place // 4) % 4, place % 4
    me2 = jnp.where(c == 0, x, y)
    a2 = (me2 + jnp.where(slot == 0, 0, jnp.where(slot == 1, 3, jnp.where(slot == 2, 1, 2)))) % 4
    held = jnp.where(c == 0, a2 * 16 + zl * 4 + a1, a1 * 16 + zl * 4 + a2)
    block = jnp.sum(jnp.where(owner[None, :] == held[:, None], jnp.arange(64)[None, :], 0), axis=1)
    column = block // 8
    target, core = column // 2, column % 2
    order = jnp.where((target == (q ^ 1)) == (core == 0), 1, 2)
    order = jnp.where(target == q, 3, jnp.where(target == (q + 2) % 4, 0, order))
    order = order + jnp.where(core == c, 4, 0)
    return (order * 8 + block % 8).astype(jnp.int32)


def project_kernel(
    places, rows, low, high, up_on, up_end, down_end, down_on, far_up, far_down, away, near, late,
    total, sems,
):
    base = 0
    for piece in (low, high, up_on, up_end, down_end, down_on, far_up, far_down):
        product = lax.dot_general(
            piece[...], rows[...], (((1,), (1,)), ((), ())), preferred_element_type=jnp.float32
        )
        for b in range(piece.shape[0] // 32):
            at = pl.multiple_of(places[base + b] * 32, 32)
            total[pl.ds(at, 32), :] = product[b * 32:(b + 1) * 32]
        base += piece.shape[0] // 32
    copies, base = [], 0
    for i, out in enumerate((away, near, late)):
        copies.append(pltpu.make_async_copy(total.at[pl.ds(base, out.shape[0])], out, sems.at[i]))
        base += out.shape[0]
    for copy in copies:
        copy.start()
    for copy in copies:
        copy.wait()


def project(places, rows, pieces):
    count = rows.shape[0]
    vmem = pl.BlockSpec(memory_space=pltpu.VMEM)
    return pl.pallas_call(
        project_kernel,
        out_shape=[
            jax.ShapeDtypeStruct((size, count), jnp.float32) for size in (1024, 512, 512)
        ],
        in_specs=[pl.BlockSpec(memory_space=pltpu.SMEM)] + [vmem] * 9,
        out_specs=[pl.BlockSpec(memory_space=pl.ANY)] * 3,
        scratch_shapes=[
            pltpu.VMEM((2048, count), jnp.float32),
            pltpu.SemaphoreType.DMA((3,)),
        ],
        compiler_params=pltpu.CompilerParams(vmem_limit_bytes=16 * 2**20),
        cost_estimate=pl.CostEstimate(flops=40_000_000_000, bytes_accessed=6000000, transcendentals=0),
        name="project",
    )(places, rows, *pieces)


def reduce_columns(arrived, away, near, late):
    got = core_swap(away)
    got_far = z_exchange(near[:256] + got[:256], 1)
    got_near = z_exchange(near[256:] + got[256:512], 1)
    second, here = lax.optimization_barrier((late[:256] + got[512:768], late[256:] + got[768:]))
    got_far, arrived = lax.optimization_barrier((got_far, arrived))
    got_late = z_exchange(second + unscaled(got_far), 2)
    here, got_late = lax.optimization_barrier((here + unscaled(got_near), got_late))
    return got, arrived, here + unscaled(got_late)


def past_kernel(table, lengths, queries, pool, arrived, scores, folded, values, cells, wide):
    steps, seqs, _ = queries.shape
    pages = pool.shape[0]

    def fetch(s, _):
        for e in range(SPAN // 16):
            entry = table[s, e]
            mine = pool[jnp.minimum(entry, pages - 1)]
            sent = arrived[jnp.maximum(entry - pages, 0)]
            cells[s, e * 16:(e + 1) * 16] = jnp.where(entry < pages, mine, sent)
        return 0

    lax.fori_loop(0, seqs, fetch, 0, unroll=2)
    cells[:, SPAN:, :] = jnp.zeros((seqs, WIDE - SPAN, cells.shape[2]), cells.dtype)
    for t in range(steps):
        for h in range(8):
            wide[h, pl.ds(t * seqs, seqs), :] = queries[t, :, h * HD:(h + 1) * HD].astype(jnp.float32)
    for s in range(seqs):
        folded[s] = jnp.concatenate(
            [wide[h, pl.ds(s, steps, stride=seqs), :] for h in range(8)], axis=0
        ).astype(jnp.bfloat16)
    column = lax.broadcasted_iota(jnp.int32, (64, WIDE), 1)
    for s in range(seqs):
        scores[s] = lax.dot_general(
            folded[s], cells[s, :, :HD], (((1,), (1,)), ((), ())),
            preferred_element_type=jnp.float32,
        ) * (HD ** -0.5)
    for s in range(seqs):
        live = (column < lengths[s]) | (column >= SPAN)
        scores[s] = jnp.where(live, scores[s], -jnp.inf)
    for s in range(seqs):
        values[s] = cells[s, :, HD:]


def past(table, lengths, queries, pool, arrived):
    steps, seqs, _ = queries.shape
    smem = pl.BlockSpec(memory_space=pltpu.SMEM)
    vmem = pl.BlockSpec(memory_space=pltpu.VMEM)
    return pl.pallas_call(
        past_kernel,
        out_shape=[
            jax.ShapeDtypeStruct((seqs, 64, WIDE), jnp.float32),
            jax.ShapeDtypeStruct((seqs, 64, HD), jnp.bfloat16),
            jax.ShapeDtypeStruct((seqs, WIDE, HD), jnp.bfloat16),
        ],
        in_specs=[smem, smem, vmem, vmem, vmem],
        out_specs=[vmem, vmem, vmem],
        scratch_shapes=[
            pltpu.VMEM((seqs, WIDE, 2 * HD), jnp.bfloat16),
            pltpu.VMEM((8, steps * seqs, HD), jnp.float32),
        ],
        compiler_params=pltpu.CompilerParams(vmem_limit_bytes=16 * 2**20),
        cost_estimate=pl.CostEstimate(flops=70_000_000, bytes_accessed=8_000_000, transcendentals=0),
        name="past",
    )(table, lengths, queries, pool, arrived)


def finish_kernel(*refs):
    total, scores, folded, values, new_kv, attended, wide, keys, mixed, weights, totals, own = refs
    seqs = scores.shape[0]
    steps = new_kv.shape[0]
    fresh = total[...].T.astype(jnp.bfloat16)
    for t in range(steps):
        new_kv[t] = fresh[t * seqs:(t + 1) * seqs]
    wide[0] = fresh[:, :HD].astype(jnp.float32)
    wide[1] = fresh[:, HD:].astype(jnp.float32)
    lanes = lax.broadcasted_iota(jnp.int32, (64, WIDE), 1)
    step = lax.broadcasted_iota(jnp.int32, (64, WIDE), 0) % steps
    later = (lanes - SPAN) > step
    zeros = jnp.zeros((16 - steps, HD), jnp.float32)
    keys[...] = jnp.zeros(keys.shape, keys.dtype)
    for s in range(seqs):
        key, value = (
            jnp.concatenate([wide[i, pl.ds(s, steps, stride=seqs), :], zeros], axis=0)
            for i in range(2)
        )
        keys[s, pl.ds(SPAN, 16), :] = key.astype(jnp.bfloat16)
        own[s] = value.astype(jnp.bfloat16)
    for s in range(seqs):
        recent = lax.dot_general(
            folded[s], keys[s], (((1,), (1,)), ((), ())), preferred_element_type=jnp.float32
        ) * (HD ** -0.5)
        mixed[pl.ds(s * 64, 64), :] = jnp.where(later, -jnp.inf, scores[s] + recent)
    for s in range(seqs):
        score = mixed[pl.ds(s * 64, 64), :]
        weight = jnp.exp(score - jnp.max(score, axis=1, keepdims=True))
        weights[s] = weight.astype(jnp.bfloat16)
        totals[s] = jnp.broadcast_to(jnp.sum(weight, axis=1, keepdims=True), (64, HD))
    for s in range(seqs):
        value = jnp.concatenate([values[s, :SPAN], own[s], values[s, SPAN + 16:]], axis=0)
        out = lax.dot_general(
            weights[s], value, (((1,), (0,)), ((), ())), preferred_element_type=jnp.float32
        )
        mixed[pl.ds(s * 64, 64), :] = out / totals[s]
    for t in range(steps):
        for h in range(8):
            attended[t, :, h * HD:(h + 1) * HD] = mixed[
                pl.ds(h * steps + t, seqs, stride=64), :
            ].astype(jnp.bfloat16)


def finish(total, scores, folded, values, steps):
    seqs = scores.shape[0]
    vmem = pl.BlockSpec(memory_space=pltpu.VMEM)
    return pl.pallas_call(
        finish_kernel,
        out_shape=[
            jax.ShapeDtypeStruct((steps, seqs, 2 * HD), jnp.bfloat16),
            jax.ShapeDtypeStruct((steps, seqs, 8 * HD), jnp.bfloat16),
        ],
        in_specs=[vmem] * 4,
        out_specs=[vmem, vmem],
        scratch_shapes=[
            pltpu.VMEM((2, steps * seqs, HD), jnp.float32),
            pltpu.VMEM((seqs, WIDE, HD), jnp.bfloat16),
            pltpu.VMEM((seqs * 64, HD), jnp.float32),
            pltpu.VMEM((seqs, 64, WIDE), jnp.bfloat16),
            pltpu.VMEM((seqs, 64, HD), jnp.float32),
            pltpu.VMEM((seqs, 16, HD), jnp.bfloat16),
        ],
        compiler_params=pltpu.CompilerParams(vmem_limit_bytes=16 * 2**20),
        cost_estimate=pl.CostEstimate(flops=140_000_000, bytes_accessed=4_000_000, transcendentals=262144),
        name="finish",
    )(total, scores, folded, values)


def on_device(hidden, kv_weight, owner, queries, pool, page_table, lengths, send_pages):
    steps_count, _, feature_part = hidden.shape
    page_size, kv_width = pool.shape[1:]
    c, q = lax.axis_index("c"), lax.axis_index("zh")
    outgoing = jnp.take(pool, send_pages.reshape(-1), axis=0, mode="clip").reshape(
        64, -1, page_size, kv_width
    )
    outgoing, pieces = gather_weight(kv_weight, outgoing)
    arrived = lax.all_to_all(outgoing, REPLICA, split_axis=0, concat_axis=0, tiled=True)
    places = block_places(owner, c, q)
    swapped, arrived, total = reduce_columns(arrived, *project(places, hidden.reshape(-1, feature_part), pieces))
    queries, _ = lax.optimization_barrier((queries, swapped))
    scores, folded, values = past(
        page_table, lengths, queries, pool, arrived.reshape(-1, page_size, kv_width)
    )
    return tuple(finish(total, scores, folded, values, steps_count))


def solution(mesh):
    fine = Mesh(mesh.devices.reshape(SIDE, SIDE, SIDE, SIDE, CORES), AXES)
    in_specs = (
        P(None, REPLICA, TENSOR),
        P(REPLICA, TENSOR),
        P(),
        P(None, REPLICA, TENSOR),
        P(REPLICA, None, TENSOR),
        P(REPLICA, None),
        P(REPLICA),
        P(REPLICA, None, None),
    )
    out_specs = (P(None, REPLICA, TENSOR), P(None, REPLICA, TENSOR))
    return jax.shard_map(
        on_device, mesh=fine, in_specs=in_specs, out_specs=out_specs, check_vma=False
    )
```

```python
import jax
import jax.numpy as jnp
from jax import lax
from jax.experimental import pallas as pl
from jax.experimental.pallas import tpu as pltpu
from jax.sharding import Mesh, PartitionSpec as P

HD = 128
SIDE = 4
CORES = 2
SCALE = 16.0
SPAN = 96
WIDE = 128
AXES = ("x", "zl", "y", "zh", "c")
REPLICA = ("x", "zl", "y")
TENSOR = ("zh", "c")
RING = range(SIDE)


def flat_id(x, zl, y, zh, c):
    return (((x * SIDE + zl) * SIDE + y) * SIDE + zh) * CORES + c


def member(stage, c, line, k, zl, zh):
    along_y = (c == 0) == (stage == 1)
    return flat_id(line, zl, k, zh, c) if along_y else flat_id(k, zl, line, zh, c)


def lines(stage):
    return [
        [member(stage, c, line, k, zl, zh) for k in RING]
        for line in RING for zl in RING for zh in RING for c in range(CORES)
    ]


def shift(value, stage, step):
    pairs = [
        (group[k], group[(k + step) % SIDE]) for group in lines(stage) for k in RING
    ]
    return lax.ppermute(value, AXES, pairs)


def partner(zh, c, step):
    return zh ^ 1 if (c == 0) == (step == 1) else SIDE - 1 - zh


def z_exchange(value, step):
    pairs = [
        (zh * CORES + c, partner(zh, c, step) * CORES + c) for zh in RING for c in range(CORES)
    ]
    return lax.ppermute((value * SCALE).astype(jnp.float16), TENSOR, pairs)


def unscaled(value):
    return value.astype(jnp.float32) * (1.0 / SCALE)


def core_swap(value):
    return lax.ppermute(value, "c", [(0, 1), (1, 0)])


def gather_weight(held, outgoing):
    first = lax.all_to_all(
        jnp.broadcast_to(held[None], (SIDE,) + held.shape), "zl", 0, 0, tiled=True
    )
    first, outgoing = lax.optimization_barrier((first, outgoing))
    block = first.reshape(-1, held.shape[1])
    high = jnp.concatenate([shift(block, 1, 2), shift(block, 1, -1)])
    low = jnp.concatenate([block, shift(block, 1, 1)])
    down_on, up_on = shift(high, 2, -1), shift(low, 2, 1)
    down_end, up_end = shift(low, 2, -1), shift(high, 2, 1)
    far_up, far_down = shift(up_on, 2, 1), shift(down_on, 2, -1)
    return outgoing, (low, high, up_on, up_end, down_end, down_on, far_up, far_down)


def block_places(owner, c, q):
    x, y = lax.axis_index("x"), lax.axis_index("y")
    place = jnp.arange(64)
    slot, a1, zl = place // 16, (place // 4) % 4, place % 4
    me1, me2 = jnp.where(c == 0, y, x), jnp.where(c == 0, x, y)
    turns = lambda k: jnp.where(k == 0, 0, jnp.where(k == 1, 3, jnp.where(k == 2, 1, 2)))
    a1, a2 = (me1 - a1) % SIDE, (me2 + turns(slot)) % SIDE
    held = jnp.where(c == 0, a2 * 16 + zl * 4 + a1, a1 * 16 + zl * 4 + a2)
    block = jnp.sum(jnp.where(owner[None, :] == held[:, None], jnp.arange(64)[None, :], 0), axis=1)
    column = block // 8
    target, core = column // 2, column % 2
    order = jnp.where((target == (q ^ 1)) == (core == 0), 1, 2)
    order = jnp.where(target == q, 3, jnp.where(target == (q + 2) % 4, 0, order))
    order = order + jnp.where(core == c, 4, 0)
    return (order * 8 + block % 8).astype(jnp.int32)


def project_kernel(
    places, rows, low, high, up_on, up_end, down_end, down_on, far_up, far_down, away, near, late,
    total, sems,
):
    base = 0
    for piece in (low, high, up_on, up_end, down_end, down_on, far_up, far_down):
        product = lax.dot_general(
            piece[...], rows[...], (((1,), (1,)), ((), ())), preferred_element_type=jnp.float32
        )
        for b in range(piece.shape[0] // 32):
            at = pl.multiple_of(places[base + b] * 32, 32)
            total[pl.ds(at, 32), :] = product[b * 32:(b + 1) * 32]
        base += piece.shape[0] // 32
    copies, base = [], 0
    for i, out in enumerate((away, near, late)):
        copies.append(pltpu.make_async_copy(total.at[pl.ds(base, out.shape[0])], out, sems.at[i]))
        base += out.shape[0]
    for copy in copies:
        copy.start()
    for copy in copies:
        copy.wait()


def project(places, rows, pieces):
    count = rows.shape[0]
    vmem = pl.BlockSpec(memory_space=pltpu.VMEM)
    return pl.pallas_call(
        project_kernel,
        out_shape=[
            jax.ShapeDtypeStruct((size, count), jnp.float32) for size in (1024, 512, 512)
        ],
        in_specs=[pl.BlockSpec(memory_space=pltpu.SMEM)] + [vmem] * 9,
        out_specs=[pl.BlockSpec(memory_space=pl.ANY)] * 3,
        scratch_shapes=[
            pltpu.VMEM((2048, count), jnp.float32),
            pltpu.SemaphoreType.DMA((3,)),
        ],
        compiler_params=pltpu.CompilerParams(vmem_limit_bytes=16 * 2**20),
        cost_estimate=pl.CostEstimate(flops=40_000_000_000, bytes_accessed=6000000, transcendentals=0),
        name="project",
    )(places, rows, *pieces)


def reduce_columns(arrived, away, near, late):
    got = core_swap(away)
    got_far = z_exchange(near[:256] + got[:256], 1)
    got_near = z_exchange(near[256:] + got[256:512], 1)
    second, here = lax.optimization_barrier((late[:256] + got[512:768], late[256:] + got[768:]))
    got_far, arrived = lax.optimization_barrier((got_far, arrived))
    got_late = z_exchange(second + unscaled(got_far), 2)
    here, got_late = lax.optimization_barrier((here + unscaled(got_near), got_late))
    return got, arrived, here + unscaled(got_late)


def past_kernel(table, lengths, queries, pool, arrived, scores, folded, values, cells, wide):
    steps, seqs, _ = queries.shape
    pages = pool.shape[0]

    def fetch(s, _):
        for e in range(SPAN // 16):
            entry = table[s, e]
            mine = pool[jnp.minimum(entry, pages - 1)]
            sent = arrived[jnp.maximum(entry - pages, 0)]
            cells[s, e * 16:(e + 1) * 16] = jnp.where(entry < pages, mine, sent)
        return 0

    lax.fori_loop(0, seqs, fetch, 0, unroll=2)
    cells[:, SPAN:, :] = jnp.zeros((seqs, WIDE - SPAN, cells.shape[2]), cells.dtype)
    for t in range(steps):
        for h in range(8):
            wide[h, pl.ds(t * seqs, seqs), :] = queries[t, :, h * HD:(h + 1) * HD].astype(jnp.float32)
    for s in range(seqs):
        folded[s] = jnp.concatenate(
            [wide[h, pl.ds(s, steps, stride=seqs), :] for h in range(8)], axis=0
        ).astype(jnp.bfloat16)
    column = lax.broadcasted_iota(jnp.int32, (64, WIDE), 1)
    for s in range(seqs):
        scores[s] = lax.dot_general(
            folded[s], cells[s, :, :HD], (((1,), (1,)), ((), ())),
            preferred_element_type=jnp.float32,
        ) * (HD ** -0.5)
    for s in range(seqs):
        live = (column < lengths[s]) | (column >= SPAN)
        scores[s] = jnp.where(live, scores[s], -jnp.inf)
    for s in range(seqs):
        values[s] = cells[s, :, HD:]


def past(table, lengths, queries, pool, arrived):
    steps, seqs, _ = queries.shape
    smem = pl.BlockSpec(memory_space=pltpu.SMEM)
    vmem = pl.BlockSpec(memory_space=pltpu.VMEM)
    return pl.pallas_call(
        past_kernel,
        out_shape=[
            jax.ShapeDtypeStruct((seqs, 64, WIDE), jnp.float32),
            jax.ShapeDtypeStruct((seqs, 64, HD), jnp.bfloat16),
            jax.ShapeDtypeStruct((seqs, WIDE, HD), jnp.bfloat16),
        ],
        in_specs=[smem, smem, vmem, vmem, vmem],
        out_specs=[vmem, vmem, vmem],
        scratch_shapes=[
            pltpu.VMEM((seqs, WIDE, 2 * HD), jnp.bfloat16),
            pltpu.VMEM((8, steps * seqs, HD), jnp.float32),
        ],
        compiler_params=pltpu.CompilerParams(vmem_limit_bytes=16 * 2**20),
        cost_estimate=pl.CostEstimate(flops=70_000_000, bytes_accessed=8_000_000, transcendentals=0),
        name="past",
    )(table, lengths, queries, pool, arrived)


def finish_kernel(*refs):
    total, scores, folded, values, new_kv, attended, wide, keys, mixed, weights, totals, own = refs
    seqs = scores.shape[0]
    steps = new_kv.shape[0]
    fresh = total[...].T.astype(jnp.bfloat16)
    for t in range(steps):
        new_kv[t] = fresh[t * seqs:(t + 1) * seqs]
    wide[0] = fresh[:, :HD].astype(jnp.float32)
    wide[1] = fresh[:, HD:].astype(jnp.float32)
    lanes = lax.broadcasted_iota(jnp.int32, (64, WIDE), 1)
    step = lax.broadcasted_iota(jnp.int32, (64, WIDE), 0) % steps
    later = (lanes - SPAN) > step
    zeros = jnp.zeros((16 - steps, HD), jnp.float32)
    keys[...] = jnp.zeros(keys.shape, keys.dtype)
    for s in range(seqs):
        key, value = (
            jnp.concatenate([wide[i, pl.ds(s, steps, stride=seqs), :], zeros], axis=0)
            for i in range(2)
        )
        keys[s, pl.ds(SPAN, 16), :] = key.astype(jnp.bfloat16)
        own[s] = value.astype(jnp.bfloat16)
    for s in range(seqs):
        recent = lax.dot_general(
            folded[s], keys[s], (((1,), (1,)), ((), ())), preferred_element_type=jnp.float32
        ) * (HD ** -0.5)
        mixed[pl.ds(s * 64, 64), :] = jnp.where(later, -jnp.inf, scores[s] + recent)
    for s in range(seqs):
        score = mixed[pl.ds(s * 64, 64), :]
        weight = jnp.exp(score - jnp.max(score, axis=1, keepdims=True))
        weights[s] = weight.astype(jnp.bfloat16)
        totals[s] = jnp.broadcast_to(jnp.sum(weight, axis=1, keepdims=True), (64, HD))
    for s in range(seqs):
        value = jnp.concatenate([values[s, :SPAN], own[s], values[s, SPAN + 16:]], axis=0)
        out = lax.dot_general(
            weights[s], value, (((1,), (0,)), ((), ())), preferred_element_type=jnp.float32
        )
        mixed[pl.ds(s * 64, 64), :] = out / totals[s]
    for t in range(steps):
        for h in range(8):
            attended[t, :, h * HD:(h + 1) * HD] = mixed[
                pl.ds(h * steps + t, seqs, stride=64), :
            ].astype(jnp.bfloat16)


def finish(total, scores, folded, values, steps):
    seqs = scores.shape[0]
    vmem = pl.BlockSpec(memory_space=pltpu.VMEM)
    return pl.pallas_call(
        finish_kernel,
        out_shape=[
            jax.ShapeDtypeStruct((steps, seqs, 2 * HD), jnp.bfloat16),
            jax.ShapeDtypeStruct((steps, seqs, 8 * HD), jnp.bfloat16),
        ],
        in_specs=[vmem] * 4,
        out_specs=[vmem, vmem],
        scratch_shapes=[
            pltpu.VMEM((2, steps * seqs, HD), jnp.float32),
            pltpu.VMEM((seqs, WIDE, HD), jnp.bfloat16),
            pltpu.VMEM((seqs * 64, HD), jnp.float32),
            pltpu.VMEM((seqs, 64, WIDE), jnp.bfloat16),
            pltpu.VMEM((seqs, 64, HD), jnp.float32),
            pltpu.VMEM((seqs, 16, HD), jnp.bfloat16),
        ],
        compiler_params=pltpu.CompilerParams(vmem_limit_bytes=16 * 2**20),
        cost_estimate=pl.CostEstimate(flops=140_000_000, bytes_accessed=4_000_000, transcendentals=262144),
        name="finish",
    )(total, scores, folded, values)


def on_device(hidden, kv_weight, owner, queries, pool, page_table, lengths, send_pages):
    steps_count, _, feature_part = hidden.shape
    page_size, kv_width = pool.shape[1:]
    c, q = lax.axis_index("c"), lax.axis_index("zh")
    outgoing = jnp.take(pool, send_pages.reshape(-1), axis=0, mode="clip").reshape(
        64, -1, page_size, kv_width
    )
    outgoing, pieces = gather_weight(kv_weight, outgoing)
    arrived = lax.all_to_all(outgoing, REPLICA, split_axis=0, concat_axis=0, tiled=True)
    places = block_places(owner, c, q)
    swapped, arrived, total = reduce_columns(arrived, *project(places, hidden.reshape(-1, feature_part), pieces))
    queries, _ = lax.optimization_barrier((queries, swapped))
    scores, folded, values = past(
        page_table, lengths, queries, pool, arrived.reshape(-1, page_size, kv_width)
    )
    return tuple(finish(total, scores, folded, values, steps_count))


def solution(mesh):
    fine = Mesh(mesh.devices.reshape(SIDE, SIDE, SIDE, SIDE, CORES), AXES)
    in_specs = (
        P(None, REPLICA, TENSOR),
        P(REPLICA, TENSOR),
        P(),
        P(None, REPLICA, TENSOR),
        P(REPLICA, None, TENSOR),
        P(REPLICA, None),
        P(REPLICA),
        P(REPLICA, None, None),
    )
    out_specs = (P(None, REPLICA, TENSOR), P(None, REPLICA, TENSOR))
    return jax.shard_map(
        on_device, mesh=fine, in_specs=in_specs, out_specs=out_specs, check_vma=False
    )
```

```python
import jax
import jax.numpy as jnp
from jax import lax
from jax.experimental import pallas as pl
from jax.experimental.pallas import tpu as pltpu
from jax.sharding import Mesh, PartitionSpec as P

HD = 128
SIDE = 4
CORES = 2
SPAN = 96
WIDE = 128
AXES = ("x", "zl", "y", "zh", "c")
REPLICA = ("x", "zl", "y")
TENSOR = ("zh", "c")
RING = range(SIDE)


def flat_id(x, zl, y, zh, c):
    return (((x * SIDE + zl) * SIDE + y) * SIDE + zh) * CORES + c


def member(stage, c, line, k, zl, zh):
    along_y = (c == 0) == (stage == 1)
    return flat_id(line, zl, k, zh, c) if along_y else flat_id(k, zl, line, zh, c)


def lines(stage):
    return [
        [member(stage, c, line, k, zl, zh) for k in RING]
        for line in RING for zl in RING for zh in RING for c in range(CORES)
    ]


def shift(value, stage, step):
    pairs = [
        (group[k], group[(k + step) % SIDE]) for group in lines(stage) for k in RING
    ]
    return lax.ppermute(value, AXES, pairs)


def partner(zh, c, step):
    return zh ^ 1 if (c == 0) == (step == 1) else SIDE - 1 - zh


def z_exchange(value, step):
    pairs = [
        (zh * CORES + c, partner(zh, c, step) * CORES + c) for zh in RING for c in range(CORES)
    ]
    return lax.ppermute(value, TENSOR, pairs)


def core_swap(value):
    return lax.ppermute(value, "c", [(0, 1), (1, 0)])


def gather_weight(held, outgoing):
    first = lax.all_to_all(
        jnp.broadcast_to(held[None], (SIDE,) + held.shape), "zl", 0, 0, tiled=True
    )
    first, outgoing = lax.optimization_barrier((first, outgoing))
    block = first.reshape(-1, held.shape[1])
    high = jnp.concatenate([shift(block, 1, 2), shift(block, 1, -1)])
    low = jnp.concatenate([block, shift(block, 1, 1)])
    down_on, up_on = shift(high, 2, -1), shift(low, 2, 1)
    down_end, up_end = shift(low, 2, -1), shift(high, 2, 1)
    far_up, far_down = shift(up_on, 2, 1), shift(down_on, 2, -1)
    return outgoing, (low, high, up_on, up_end, down_end, down_on, far_up, far_down)


def block_places(owner, c, q):
    x, y = lax.axis_index("x"), lax.axis_index("y")
    place = jnp.arange(64)
    slot, a1, zl = place // 16, (place // 4) % 4, place % 4
    me1, me2 = jnp.where(c == 0, y, x), jnp.where(c == 0, x, y)
    turns = lambda k: jnp.where(k == 0, 0, jnp.where(k == 1, 3, jnp.where(k == 2, 1, 2)))
    a1, a2 = (me1 - a1) % SIDE, (me2 + turns(slot)) % SIDE
    held = jnp.where(c == 0, a2 * 16 + zl * 4 + a1, a1 * 16 + zl * 4 + a2)
    block = jnp.sum(jnp.where(owner[None, :] == held[:, None], jnp.arange(64)[None, :], 0), axis=1)
    column = block // 8
    target, core = column // 2, column % 2
    order = jnp.where((target == (q ^ 1)) == (core == 0), 1, 2)
    order = jnp.where(target == q, 3, jnp.where(target == (q + 2) % 4, 0, order))
    order = order + jnp.where(core == c, 4, 0)
    return (order * 8 + block % 8).astype(jnp.int32)


def project_kernel(
    places, rows, low, high, up_on, up_end, down_end, down_on, far_up, far_down, away, near, late,
    total, sems,
):
    base = 0
    for piece in (low, high, up_on, up_end, down_end, down_on, far_up, far_down):
        product = lax.dot_general(
            piece[...], rows[...], (((1,), (1,)), ((), ())), preferred_element_type=jnp.float32
        )
        for b in range(piece.shape[0] // 32):
            at = pl.multiple_of(places[base + b] * 32, 32)
            total[pl.ds(at, 32), :] = product[b * 32:(b + 1) * 32]
        base += piece.shape[0] // 32
    copies, base = [], 0
    for i, out in enumerate((away, near, late)):
        copies.append(pltpu.make_async_copy(total.at[pl.ds(base, out.shape[0])], out, sems.at[i]))
        base += out.shape[0]
    for copy in copies:
        copy.start()
    for copy in copies:
        copy.wait()


def project(places, rows, pieces):
    count = rows.shape[0]
    vmem = pl.BlockSpec(memory_space=pltpu.VMEM)
    return pl.pallas_call(
        project_kernel,
        out_shape=[
            jax.ShapeDtypeStruct((size, count), jnp.float32) for size in (1024, 512, 512)
        ],
        in_specs=[pl.BlockSpec(memory_space=pltpu.SMEM)] + [vmem] * 9,
        out_specs=[pl.BlockSpec(memory_space=pl.ANY)] * 3,
        scratch_shapes=[
            pltpu.VMEM((2048, count), jnp.float32),
            pltpu.SemaphoreType.DMA((3,)),
        ],
        compiler_params=pltpu.CompilerParams(vmem_limit_bytes=16 * 2**20),
        cost_estimate=pl.CostEstimate(flops=40_000_000_000, bytes_accessed=6000000, transcendentals=0),
        name="project",
    )(places, rows, *pieces)


def reduce_columns(arrived, away, near, late):
    got = core_swap(away)
    got_far = z_exchange(near[:256] + got[:256], 1)
    got_near = z_exchange(near[256:] + got[256:512], 1)
    second, here = lax.optimization_barrier((late[:256] + got[512:768], late[256:] + got[768:]))
    got_far, arrived = lax.optimization_barrier((got_far, arrived))
    got_late = z_exchange(second + got_far, 2)
    here, got_late = lax.optimization_barrier((here + got_near, got_late))
    return got, arrived, here + got_late


def past_kernel(table, lengths, queries, pool, arrived, scores, folded, values, cells, wide):
    steps, seqs, _ = queries.shape
    pages = pool.shape[0]

    def fetch(s, _):
        for e in range(SPAN // 16):
            entry = table[s, e]
            mine = pool[jnp.minimum(entry, pages - 1)]
            sent = arrived[jnp.maximum(entry - pages, 0)]
            cells[s, e * 16:(e + 1) * 16] = jnp.where(entry < pages, mine, sent)
        return 0

    lax.fori_loop(0, seqs, fetch, 0, unroll=2)
    cells[:, SPAN:, :] = jnp.zeros((seqs, WIDE - SPAN, cells.shape[2]), cells.dtype)
    for t in range(steps):
        for h in range(8):
            wide[h, pl.ds(t * seqs, seqs), :] = queries[t, :, h * HD:(h + 1) * HD].astype(jnp.float32)
    for s in range(seqs):
        folded[s] = jnp.concatenate(
            [wide[h, pl.ds(s, steps, stride=seqs), :] for h in range(8)], axis=0
        ).astype(jnp.bfloat16)
    column = lax.broadcasted_iota(jnp.int32, (64, WIDE), 1)
    for s in range(seqs):
        scores[s] = lax.dot_general(
            folded[s], cells[s, :, :HD], (((1,), (1,)), ((), ())),
            preferred_element_type=jnp.float32,
        ) * (HD ** -0.5)
    for s in range(seqs):
        live = (column < lengths[s]) | (column >= SPAN)
        scores[s] = jnp.where(live, scores[s], -jnp.inf)
    for s in range(seqs):
        values[s] = cells[s, :, HD:]


def past(table, lengths, queries, pool, arrived):
    steps, seqs, _ = queries.shape
    smem = pl.BlockSpec(memory_space=pltpu.SMEM)
    vmem = pl.BlockSpec(memory_space=pltpu.VMEM)
    return pl.pallas_call(
        past_kernel,
        out_shape=[
            jax.ShapeDtypeStruct((seqs, 64, WIDE), jnp.float32),
            jax.ShapeDtypeStruct((seqs, 64, HD), jnp.bfloat16),
            jax.ShapeDtypeStruct((seqs, WIDE, HD), jnp.bfloat16),
        ],
        in_specs=[smem, smem, vmem, vmem, vmem],
        out_specs=[vmem, vmem, vmem],
        scratch_shapes=[
            pltpu.VMEM((seqs, WIDE, 2 * HD), jnp.bfloat16),
            pltpu.VMEM((8, steps * seqs, HD), jnp.float32),
        ],
        compiler_params=pltpu.CompilerParams(vmem_limit_bytes=16 * 2**20),
        cost_estimate=pl.CostEstimate(flops=70_000_000, bytes_accessed=8_000_000, transcendentals=0),
        name="past",
    )(table, lengths, queries, pool, arrived)


def finish_kernel(*refs):
    total, scores, folded, values, new_kv, attended, wide, keys, mixed, weights, totals, own = refs
    seqs = scores.shape[0]
    steps = new_kv.shape[0]
    fresh = total[...].T.astype(jnp.bfloat16)
    for t in range(steps):
        new_kv[t] = fresh[t * seqs:(t + 1) * seqs]
    wide[0] = fresh[:, :HD].astype(jnp.float32)
    wide[1] = fresh[:, HD:].astype(jnp.float32)
    lanes = lax.broadcasted_iota(jnp.int32, (64, WIDE), 1)
    step = lax.broadcasted_iota(jnp.int32, (64, WIDE), 0) % steps
    later = (lanes - SPAN) > step
    zeros = jnp.zeros((16 - steps, HD), jnp.float32)
    keys[...] = jnp.zeros(keys.shape, keys.dtype)
    for s in range(seqs):
        key, value = (
            jnp.concatenate([wide[i, pl.ds(s, steps, stride=seqs), :], zeros], axis=0)
            for i in range(2)
        )
        keys[s, pl.ds(SPAN, 16), :] = key.astype(jnp.bfloat16)
        own[s] = value.astype(jnp.bfloat16)
    for s in range(seqs):
        recent = lax.dot_general(
            folded[s], keys[s], (((1,), (1,)), ((), ())), preferred_element_type=jnp.float32
        ) * (HD ** -0.5)
        mixed[pl.ds(s * 64, 64), :] = jnp.where(later, -jnp.inf, scores[s] + recent)
    for s in range(seqs):
        score = mixed[pl.ds(s * 64, 64), :]
        weight = jnp.exp(score - jnp.max(score, axis=1, keepdims=True))
        weights[s] = weight.astype(jnp.bfloat16)
        totals[s] = jnp.broadcast_to(jnp.sum(weight, axis=1, keepdims=True), (64, HD))
    for s in range(seqs):
        value = jnp.concatenate([values[s, :SPAN], own[s], values[s, SPAN + 16:]], axis=0)
        out = lax.dot_general(
            weights[s], value, (((1,), (0,)), ((), ())), preferred_element_type=jnp.float32
        )
        mixed[pl.ds(s * 64, 64), :] = out / totals[s]
    for t in range(steps):
        for h in range(8):
            attended[t, :, h * HD:(h + 1) * HD] = mixed[
                pl.ds(h * steps + t, seqs, stride=64), :
            ].astype(jnp.bfloat16)


def finish(total, scores, folded, values, steps):
    seqs = scores.shape[0]
    vmem = pl.BlockSpec(memory_space=pltpu.VMEM)
    return pl.pallas_call(
        finish_kernel,
        out_shape=[
            jax.ShapeDtypeStruct((steps, seqs, 2 * HD), jnp.bfloat16),
            jax.ShapeDtypeStruct((steps, seqs, 8 * HD), jnp.bfloat16),
        ],
        in_specs=[vmem] * 4,
        out_specs=[vmem, vmem],
        scratch_shapes=[
            pltpu.VMEM((2, steps * seqs, HD), jnp.float32),
            pltpu.VMEM((seqs, WIDE, HD), jnp.bfloat16),
            pltpu.VMEM((seqs * 64, HD), jnp.float32),
            pltpu.VMEM((seqs, 64, WIDE), jnp.bfloat16),
            pltpu.VMEM((seqs, 64, HD), jnp.float32),
            pltpu.VMEM((seqs, 16, HD), jnp.bfloat16),
        ],
        compiler_params=pltpu.CompilerParams(vmem_limit_bytes=16 * 2**20),
        cost_estimate=pl.CostEstimate(flops=140_000_000, bytes_accessed=4_000_000, transcendentals=262144),
        name="finish",
    )(total, scores, folded, values)


def on_device(hidden, kv_weight, owner, queries, pool, page_table, lengths, send_pages):
    steps_count, _, feature_part = hidden.shape
    page_size, kv_width = pool.shape[1:]
    c, q = lax.axis_index("c"), lax.axis_index("zh")
    outgoing = jnp.take(pool, send_pages.reshape(-1), axis=0, mode="clip").reshape(
        64, -1, page_size, kv_width
    )
    outgoing, pieces = gather_weight(kv_weight, outgoing)
    arrived = lax.all_to_all(outgoing, REPLICA, split_axis=0, concat_axis=0, tiled=True)
    places = block_places(owner, c, q)
    swapped, arrived, total = reduce_columns(arrived, *project(places, hidden.reshape(-1, feature_part), pieces))
    queries, _ = lax.optimization_barrier((queries, swapped))
    scores, folded, values = past(
        page_table, lengths, queries, pool, arrived.reshape(-1, page_size, kv_width)
    )
    return tuple(finish(total, scores, folded, values, steps_count))


def solution(mesh):
    fine = Mesh(mesh.devices.reshape(SIDE, SIDE, SIDE, SIDE, CORES), AXES)
    in_specs = (
        P(None, REPLICA, TENSOR),
        P(REPLICA, TENSOR),
        P(),
        P(None, REPLICA, TENSOR),
        P(REPLICA, None, TENSOR),
        P(REPLICA, None),
        P(REPLICA),
        P(REPLICA, None, None),
    )
    out_specs = (P(None, REPLICA, TENSOR), P(None, REPLICA, TENSOR))
    return jax.shard_map(
        on_device, mesh=fine, in_specs=in_specs, out_specs=out_specs, check_vma=False
    )
```

```python
import jax
import jax.numpy as jnp
from jax import lax
from jax.experimental import pallas as pl
from jax.experimental.pallas import tpu as pltpu
from jax.sharding import Mesh, PartitionSpec as P

HD = 128
SIDE = 4
CORES = 2
SCALE = 16.0
SPAN = 96
WIDE = 128
AXES = ("x", "zl", "y", "zh", "c")
REPLICA = ("x", "zl", "y")
TENSOR = ("zh", "c")
RING = range(SIDE)


def flat_id(x, zl, y, zh, c):
    return (((x * SIDE + zl) * SIDE + y) * SIDE + zh) * CORES + c


def member(stage, c, line, k, zl, zh):
    along_y = (c == 0) == (stage == 1)
    return flat_id(line, zl, k, zh, c) if along_y else flat_id(k, zl, line, zh, c)


def lines(stage):
    return [
        [member(stage, c, line, k, zl, zh) for k in RING]
        for line in RING for zl in RING for zh in RING for c in range(CORES)
    ]


def shift(value, stage, step):
    pairs = [
        (group[k], group[(k + step) % SIDE]) for group in lines(stage) for k in RING
    ]
    return lax.ppermute(value, AXES, pairs)


def partner(zh, c, step):
    return zh ^ 1 if (c == 0) == (step == 1) else SIDE - 1 - zh


def z_exchange(value, step):
    pairs = [
        (zh * CORES + c, partner(zh, c, step) * CORES + c) for zh in RING for c in range(CORES)
    ]
    return lax.ppermute((value * SCALE).astype(jnp.float16), TENSOR, pairs)


def unscaled(value):
    return value.astype(jnp.float32) * (1.0 / SCALE)


def core_swap(value):
    return lax.ppermute(value, "c", [(0, 1), (1, 0)])


def gather_weight(held, outgoing):
    first = lax.all_to_all(
        jnp.broadcast_to(held[None], (SIDE,) + held.shape), "zl", 0, 0, tiled=True
    )
    first, outgoing = lax.optimization_barrier((first, outgoing))
    block = first.reshape(-1, held.shape[1])
    high = jnp.concatenate([shift(block, 1, 2), shift(block, 1, -1)])
    low = jnp.concatenate([block, shift(block, 1, 1)])
    down_on, up_on = shift(high, 2, -1), shift(low, 2, 1)
    down_end, up_end = shift(low, 2, -1), shift(high, 2, 1)
    far_up, far_down = shift(up_on, 2, 1), shift(down_on, 2, -1)
    return outgoing, (low, high, up_on, up_end, down_end, down_on, far_up, far_down)


def block_places(owner, c, q):
    x, y = lax.axis_index("x"), lax.axis_index("y")
    place = jnp.arange(64)
    slot, a1, zl = place // 16, (place // 4) % 4, place % 4
    me1, me2 = jnp.where(c == 0, y, x), jnp.where(c == 0, x, y)
    turns = lambda k: jnp.where(k == 0, 0, jnp.where(k == 1, 3, jnp.where(k == 2, 1, 2)))
    a1, a2 = (me1 - a1) % SIDE, (me2 + turns(slot)) % SIDE
    held = jnp.where(c == 0, a2 * 16 + zl * 4 + a1, a1 * 16 + zl * 4 + a2)
    block = jnp.sum(jnp.where(owner[None, :] == held[:, None], jnp.arange(64)[None, :], 0), axis=1)
    column = block // 8
    target, core = column // 2, column % 2
    order = jnp.where((target == (q ^ 1)) == (core == 0), 1, 2)
    order = jnp.where(target == q, 3, jnp.where(target == (q + 2) % 4, 0, order))
    order = order + jnp.where(core == c, 4, 0)
    return (order * 8 + block % 8).astype(jnp.int32)


def project_kernel(
    places, rows, low, high, up_on, up_end, down_end, down_on, far_up, far_down, away, near, late,
    total, sems,
):
    base = 0
    for piece in (low, high, up_on, up_end, down_end, down_on, far_up, far_down):
        product = lax.dot_general(
            piece[...], rows[...], (((1,), (1,)), ((), ())), preferred_element_type=jnp.float32
        )
        for b in range(piece.shape[0] // 32):
            at = pl.multiple_of(places[base + b] * 32, 32)
            total[pl.ds(at, 32), :] = product[b * 32:(b + 1) * 32]
        base += piece.shape[0] // 32
    copies, base = [], 0
    for i, out in enumerate((away, near, late)):
        copies.append(pltpu.make_async_copy(total.at[pl.ds(base, out.shape[0])], out, sems.at[i]))
        base += out.shape[0]
    for copy in copies:
        copy.start()
    for copy in copies:
        copy.wait()


def project(places, rows, pieces):
    count = rows.shape[0]
    vmem = pl.BlockSpec(memory_space=pltpu.VMEM)
    return pl.pallas_call(
        project_kernel,
        out_shape=[
            jax.ShapeDtypeStruct((size, count), jnp.float32) for size in (1024, 512, 512)
        ],
        in_specs=[pl.BlockSpec(memory_space=pltpu.SMEM)] + [vmem] * 9,
        out_specs=[pl.BlockSpec(memory_space=pl.ANY)] * 3,
        scratch_shapes=[
            pltpu.VMEM((2048, count), jnp.float32),
            pltpu.SemaphoreType.DMA((3,)),
        ],
        compiler_params=pltpu.CompilerParams(vmem_limit_bytes=16 * 2**20),
        cost_estimate=pl.CostEstimate(flops=40_000_000_000, bytes_accessed=6000000, transcendentals=0),
        name="project",
    )(places, rows, *pieces)


def reduce_columns(arrived, away, near, late):
    got = core_swap(away)
    got_far = z_exchange(near[:256] + got[:256], 1)
    got_near = z_exchange(near[256:] + got[256:512], 1)
    second, here = lax.optimization_barrier((late[:256] + got[512:768], late[256:] + got[768:]))
    got_far, arrived = lax.optimization_barrier((got_far, arrived))
    got_late = z_exchange(second + unscaled(got_far), 2)
    here, got_late = lax.optimization_barrier((here + unscaled(got_near), got_late))
    return got, arrived, here + unscaled(got_late)


def past_kernel(table, lengths, queries, pool, arrived, scores, folded, values, cells, wide):
    steps, seqs, _ = queries.shape
    pages = pool.shape[0]

    def fetch(s, _):
        for e in range(SPAN // 16):
            entry = table[s, e]
            mine = pool[jnp.minimum(entry, pages - 1)]
            sent = arrived[jnp.maximum(entry - pages, 0)]
            cells[s, e * 16:(e + 1) * 16] = jnp.where(entry < pages, mine, sent)
        return 0

    lax.fori_loop(0, seqs, fetch, 0, unroll=2)
    cells[:, SPAN:, :] = jnp.zeros((seqs, WIDE - SPAN, cells.shape[2]), cells.dtype)
    for t in range(steps):
        for h in range(8):
            wide[h, pl.ds(t * seqs, seqs), :] = queries[t, :, h * HD:(h + 1) * HD].astype(jnp.float32)
    for s in range(seqs):
        folded[s] = jnp.concatenate(
            [wide[h, pl.ds(s, steps, stride=seqs), :] for h in range(8)], axis=0
        ).astype(jnp.bfloat16)
    column = lax.broadcasted_iota(jnp.int32, (64, WIDE), 1)
    for s in range(seqs):
        scores[s] = lax.dot_general(
            folded[s], cells[s, :, :HD], (((1,), (1,)), ((), ())),
            preferred_element_type=jnp.float32,
        ) * (HD ** -0.5)
    for s in range(seqs):
        live = (column < lengths[s]) | (column >= SPAN)
        scores[s] = jnp.where(live, scores[s], -jnp.inf)
    for s in range(seqs):
        values[s] = cells[s, :, HD:]


def past(table, lengths, queries, pool, arrived):
    steps, seqs, _ = queries.shape
    smem = pl.BlockSpec(memory_space=pltpu.SMEM)
    vmem = pl.BlockSpec(memory_space=pltpu.VMEM)
    return pl.pallas_call(
        past_kernel,
        out_shape=[
            jax.ShapeDtypeStruct((seqs, 64, WIDE), jnp.float32),
            jax.ShapeDtypeStruct((seqs, 64, HD), jnp.bfloat16),
            jax.ShapeDtypeStruct((seqs, WIDE, HD), jnp.bfloat16),
        ],
        in_specs=[smem, smem, vmem, vmem, vmem],
        out_specs=[vmem, vmem, vmem],
        scratch_shapes=[
            pltpu.VMEM((seqs, WIDE, 2 * HD), jnp.bfloat16),
            pltpu.VMEM((8, steps * seqs, HD), jnp.float32),
        ],
        compiler_params=pltpu.CompilerParams(vmem_limit_bytes=16 * 2**20),
        cost_estimate=pl.CostEstimate(flops=70_000_000, bytes_accessed=8_000_000, transcendentals=0),
        name="past",
    )(table, lengths, queries, pool, arrived)


def finish_kernel(*refs):
    total, scores, folded, values, new_kv, attended, wide, keys, mixed, weights, totals, own = refs
    seqs = scores.shape[0]
    steps = new_kv.shape[0]
    fresh = total[...].T.astype(jnp.bfloat16)
    for t in range(steps):
        new_kv[t] = fresh[t * seqs:(t + 1) * seqs]
    wide[0] = fresh[:, :HD].astype(jnp.float32)
    wide[1] = fresh[:, HD:].astype(jnp.float32)
    lanes = lax.broadcasted_iota(jnp.int32, (64, WIDE), 1)
    step = lax.broadcasted_iota(jnp.int32, (64, WIDE), 0) % steps
    later = (lanes - SPAN) > step
    zeros = jnp.zeros((16 - steps, HD), jnp.float32)
    keys[...] = jnp.zeros(keys.shape, keys.dtype)
    for s in range(seqs):
        key, value = (
            jnp.concatenate([wide[i, pl.ds(s, steps, stride=seqs), :], zeros], axis=0)
            for i in range(2)
        )
        keys[s, pl.ds(SPAN, 16), :] = key.astype(jnp.bfloat16)
        own[s] = value.astype(jnp.bfloat16)
    for s in range(seqs):
        recent = lax.dot_general(
            folded[s], keys[s], (((1,), (1,)), ((), ())), preferred_element_type=jnp.float32
        ) * (HD ** -0.5)
        mixed[pl.ds(s * 64, 64), :] = jnp.where(later, -jnp.inf, scores[s] + recent)
    for s in range(seqs):
        score = mixed[pl.ds(s * 64, 64), :]
        weight = jnp.exp(score - jnp.max(score, axis=1, keepdims=True))
        weights[s] = weight.astype(jnp.bfloat16)
        totals[s] = jnp.broadcast_to(jnp.sum(weight, axis=1, keepdims=True), (64, HD))
    for s in range(seqs):
        value = jnp.concatenate([values[s, :SPAN], own[s], values[s, SPAN + 16:]], axis=0)
        out = lax.dot_general(
            weights[s], value, (((1,), (0,)), ((), ())), preferred_element_type=jnp.float32
        )
        mixed[pl.ds(s * 64, 64), :] = out / totals[s]
    for t in range(steps):
        for h in range(8):
            attended[t, :, h * HD:(h + 1) * HD] = mixed[
                pl.ds(h * steps + t, seqs, stride=64), :
            ].astype(jnp.bfloat16)


def finish(total, scores, folded, values, steps):
    seqs = scores.shape[0]
    vmem = pl.BlockSpec(memory_space=pltpu.VMEM)
    return pl.pallas_call(
        finish_kernel,
        out_shape=[
            jax.ShapeDtypeStruct((steps, seqs, 2 * HD), jnp.bfloat16),
            jax.ShapeDtypeStruct((steps, seqs, 8 * HD), jnp.bfloat16),
        ],
        in_specs=[vmem] * 4,
        out_specs=[vmem, vmem],
        scratch_shapes=[
            pltpu.VMEM((2, steps * seqs, HD), jnp.float32),
            pltpu.VMEM((seqs, WIDE, HD), jnp.bfloat16),
            pltpu.VMEM((seqs * 64, HD), jnp.float32),
            pltpu.VMEM((seqs, 64, WIDE), jnp.bfloat16),
            pltpu.VMEM((seqs, 64, HD), jnp.float32),
            pltpu.VMEM((seqs, 16, HD), jnp.bfloat16),
        ],
        compiler_params=pltpu.CompilerParams(vmem_limit_bytes=16 * 2**20),
        cost_estimate=pl.CostEstimate(flops=140_000_000, bytes_accessed=4_000_000, transcendentals=262144),
        name="finish",
    )(total, scores, folded, values)


def on_device(hidden, kv_weight, owner, queries, pool, page_table, lengths, send_pages):
    steps_count, _, feature_part = hidden.shape
    page_size, kv_width = pool.shape[1:]
    c, q = lax.axis_index("c"), lax.axis_index("zh")
    outgoing = jnp.take(pool, send_pages.reshape(-1), axis=0, mode="clip").reshape(-1, kv_width)
    outgoing, pieces = gather_weight(kv_weight, outgoing)
    arrived = lax.all_to_all(outgoing, REPLICA, split_axis=0, concat_axis=0, tiled=True)
    places = block_places(owner, c, q)
    swapped, arrived, total = reduce_columns(arrived, *project(places, hidden.reshape(-1, feature_part), pieces))
    queries, _ = lax.optimization_barrier((queries, swapped))
    scores, folded, values = past(
        page_table, lengths, queries, pool, arrived.reshape(-1, page_size, kv_width)
    )
    return tuple(finish(total, scores, folded, values, steps_count))


def solution(mesh):
    fine = Mesh(mesh.devices.reshape(SIDE, SIDE, SIDE, SIDE, CORES), AXES)
    in_specs = (
        P(None, REPLICA, TENSOR),
        P(REPLICA, TENSOR),
        P(),
        P(None, REPLICA, TENSOR),
        P(REPLICA, None, TENSOR),
        P(REPLICA, None),
        P(REPLICA),
        P(REPLICA, None, None),
    )
    out_specs = (P(None, REPLICA, TENSOR), P(None, REPLICA, TENSOR))
    return jax.shard_map(
        on_device, mesh=fine, in_specs=in_specs, out_specs=out_specs, check_vma=False
    )
```
